32 devices in a mesh: sx: 8 (over y, x, core), sy: 4 (over z).
Axes of the slice: x: 2, y: 2, z: 4, core: 2. Of those that a mesh axis runs over, the one named last changes fastest.
Arguments:
- tokens: bfloat16 [16384, 1024], P(('sx', 'sy')), may hold values from -6 to 6
- norm_gain: float32 [1024], replicated, may hold values from 0.1 to 1.9
- w_qk: bfloat16 [1024, 1024], replicated, may hold values from -1.75 to 1.75
- w_value: bfloat16 [1024, 1024], replicated, may hold values from -0.1875 to 0.1875
- w_out: bfloat16 [1024, 1024], replicated, may hold values from -0.1875 to 0.1875
- send_order: int32 [8, 16384], P(None, ('sx', 'sy')), may hold values from 0 to 511, as said below
- place: int32 [8, 16384], P(None, ('sx', 'sy')), may hold values from 0 to 511, as said below
Outputs:
- attended: bfloat16 [16384, 1024], P(('sx', 'sy'))
The draws below stay inside these ranges and needn't reach their ends.
Inputs may be any that keep to these rules, and one draw needn't show every extreme that they name: `send_order`: for every head and every device, the device's 512 entries form a permutation of 0 to 511. `place`: for every head and every device, the device's 512 entries form a permutation of 0 to 511.
All inputs are finite; a program needn't handle non-finite values.
Results may differ from the reference program's by a relative error of at most 0.012.
The reference program's roundings to bfloat16 on the way count: a program that leaves them out, or rounds other values in their place, can miss the bound.
Values may be sent and summed in bfloat16 or wider, within the bound.
No kernel may reach another device: no remote copies, remote signals or barrier semaphores. Data moves between devices by JAX's collectives and lax.ppermute only.
A program may use at most 64 MiB of HBM per device.

```python
import jax
import jax.numpy as jnp
from jax import lax

D = 1024
HEADS = 8
HEAD_DIM = 128
SPAN = 128
TOK_DEV = 512
TOKENS = 16384
N_SX = 8
N_SY = 4


def block_permutations(key):
    keys = jax.random.split(key, HEADS * N_SX * N_SY)
    perms = jax.vmap(lambda single: jax.random.permutation(single, TOK_DEV))(keys)
    return perms.reshape(HEADS, TOKENS).astype(jnp.int32)


def draw_send_order(key, part):
    return block_permutations(jax.random.fold_in(key, 11))


def draw_place(key, part):
    return block_permutations(jax.random.fold_in(key, 23))


def draw_w_qk(key, part):
    sigma = (D // 64) ** (-0.5)
    base = jax.random.normal(jax.random.fold_in(key, 53), (D, D), dtype=jnp.float32) * sigma
    base = jnp.clip(base, -6.0 * sigma, 6.0 * sigma)
    return base.astype(jnp.bfloat16)


def draw_tokens(key, part):
    noise = jax.random.normal(jax.random.fold_in(key, 61), (TOKENS, D), dtype=jnp.float32)
    noise = jnp.clip(noise, -6.0, 6.0)
    return noise.astype(jnp.bfloat16)


def gaussian(own_key, extent, width, reach, kind=jnp.bfloat16):
    drawn = width * jax.random.normal(own_key, extent, jnp.float32)
    return jnp.clip(drawn, min=-reach, max=reach).astype(kind)


def setup_inputs(seed: int = 0) -> dict:
    streams_of = jax.random.split(jax.random.key(seed), 8)
    return {
        "tokens": draw_tokens(jax.random.fold_in(streams_of[7], 71), 0),
        "norm_gain": jnp.clip(1.0 + 0.18 * jax.random.normal(streams_of[1], (D,), jnp.float32), 0.1, 1.9),
        "w_qk": draw_w_qk(jax.random.fold_in(streams_of[7], 71), 0),
        "w_value": gaussian(streams_of[3], (D, D), D ** -0.5, 0.1875),
        "w_out": gaussian(streams_of[4], (D, D), D ** -0.5, 0.1875),
        "send_order": draw_send_order(jax.random.fold_in(streams_of[7], 71), 0),
        "place": draw_place(jax.random.fold_in(streams_of[7], 71), 0),
    }


def bucket_order(send_order, place):
    ndev = N_SX * N_SY
    peer = TOK_DEV // ndev
    sent = send_order.reshape(HEADS, ndev, ndev, peer)
    source = sent + (jnp.arange(ndev, dtype=jnp.int32) * TOK_DEV)[None, :, None, None]
    source = source.transpose(0, 2, 1, 3).reshape(HEADS, TOKENS)
    target = place.reshape(HEADS, ndev, TOK_DEV) + (jnp.arange(ndev, dtype=jnp.int32) * TOK_DEV)[None, :, None]
    target = target.reshape(HEADS, TOKENS)
    heads_idx = jnp.arange(HEADS, dtype=jnp.int32)[:, None]
    return jnp.zeros((HEADS, TOKENS), jnp.int32).at[heads_idx, target].set(source)

def attend_spans(current, previous):
    window = jnp.concatenate([previous, current], axis=1)
    query = current[..., :HEAD_DIM].astype(jnp.float32)
    keys = window[..., :HEAD_DIM].astype(jnp.float32)
    key_stat = lax.optimization_barrier(jnp.sum(keys * keys, -1, keepdims=True)) + 1e-06
    unit = (keys * lax.rsqrt(key_stat)).astype(jnp.bfloat16)
    scores = jnp.einsum('cqd,ckd->cqk', query, unit.astype(jnp.float32)) * HEAD_DIM ** (-0.5)
    rows = jnp.arange(SPAN)[:, None]
    cols = jnp.arange(2 * SPAN)[None, :]
    scores = jnp.where(cols == rows + SPAN, -100000.0, scores)
    weights = jax.nn.softmax(scores, axis=-1).astype(jnp.bfloat16)
    vals = window[..., HEAD_DIM:].astype(jnp.float32)
    return jnp.einsum('cqk,ckd->cqd', weights.astype(jnp.float32), vals).astype(jnp.bfloat16)

def reference(tokens, norm_gain, w_qk, w_value, w_out, send_order, place):
    floats = tokens.astype(jnp.float32)
    row_stat = lax.optimization_barrier(jnp.mean(floats * floats, -1, keepdims=True)) + 1e-06
    scale = lax.rsqrt(row_stat)
    normed = (floats * scale * norm_gain.astype(jnp.float32)).astype(jnp.bfloat16)
    shared = jnp.dot(normed, w_qk, preferred_element_type=jnp.float32).astype(jnp.bfloat16)
    values = jnp.dot(normed, w_value, preferred_element_type=jnp.float32).astype(jnp.bfloat16)
    stacked = jnp.concatenate([shared.reshape(TOKENS, HEADS, HEAD_DIM), values.reshape(TOKENS, HEADS, HEAD_DIM)], -1)
    stacked = stacked.transpose(1, 0, 2)
    order = bucket_order(send_order, place)

    def one_head(pair):
        rows, index = pair
        ordered = rows[index].reshape(TOKENS // SPAN, SPAN, 2 * HEAD_DIM)
        previous = jnp.roll(ordered, 1, axis=0)
        result = attend_spans(ordered, previous).reshape(TOKENS, HEAD_DIM)
        return jnp.zeros((TOKENS, HEAD_DIM), jnp.bfloat16).at[index].set(result)
    heads_out = lax.map(one_head, (stacked, order))
    merged = heads_out.transpose(1, 0, 2).reshape(TOKENS, D)
    return jnp.dot(merged, w_out, preferred_element_type=jnp.float32).astype(jnp.bfloat16)
```

```python
import functools

import jax
import jax.numpy as jnp
from jax import lax
from jax.experimental import pallas as pl
from jax.experimental.pallas import tpu as pltpu
from jax.sharding import PartitionSpec as P

HEADS = 8
HEAD_DIM = 128
SPAN = 128
WIDTH = 2 * HEAD_DIM
AXES = ("sx", "sy")
BLOCKS_ALONG = ("sy", "sx")
MIB = 1024 * 1024
LONG = 10**12
BF16 = jnp.bfloat16
F32 = jnp.float32
ANY = pl.BlockSpec(memory_space=pl.ANY)
HBM = pl.BlockSpec(memory_space=pltpu.HBM)
VMEM = pl.BlockSpec(memory_space=pltpu.VMEM)


def dot(a, b):
    return jnp.dot(a, b, preferred_element_type=F32)


def by_column(column, size):
    lanes = lax.broadcasted_iota(jnp.int32, (column.shape[0], size), 1)
    return jnp.where(lanes == column, 1.0, 0.0).astype(BF16)


def by_row(row, first, size):
    sublanes = lax.broadcasted_iota(jnp.int32, (size, row.shape[1]), 0) + first
    return jnp.where(sublanes == row, 1.0, 0.0).astype(BF16)


def rolled(table, by):
    return pltpu.roll(table, by % table.shape[1], 1)


def relative(table, peer):
    lanes = lax.broadcasted_iota(jnp.int32, table.shape, 1)
    me = (lax.axis_index("sy") * lax.axis_size("sx") + lax.axis_index("sx")) * peer
    bit = peer
    while bit < table.shape[1]:
        other = jnp.where((lanes & bit) == 0, rolled(table, -bit), rolled(table, bit))
        table = jnp.where((me & bit) > 0, other, table)
        bit *= 2
    return table


def axes_swapped(table, minor, peer):
    lanes = lax.broadcasted_iota(jnp.int32, table.shape, 1)
    minor_bits = lax.axis_size(minor).bit_length() - 1
    major_bits = (table.shape[1] // peer).bit_length() - 1 - minor_bits
    now = list(range(major_bits + minor_bits))
    goal = [major_bits + j for j in range(minor_bits)] + list(range(major_bits))
    for j in range(len(goal)):
        if now[j] == goal[j]:
            continue
        low, high = sorted((now[j], goal[j]))
        low_bit, high_bit = peer << low, peer << high
        has_low, has_high = (lanes & low_bit) > 0, (lanes & high_bit) > 0
        down = rolled(table, low_bit - high_bit)
        up = rolled(table, high_bit - low_bit)
        table = jnp.where(has_low == has_high, table, jnp.where(has_low, down, up))
        now = [{low: high, high: low}.get(v, v) for v in now]
    return table


def to_columns(table):
    filler = jnp.zeros((128 - table.shape[0], table.shape[1]), table.dtype)
    return jnp.concatenate([table, filler], 0).T


def call(body, outs, scratch=(), specs=None, out_specs=None, cost=0, limit=40, after=()):
    count = [0]

    def skipping(*refs):
        return body(*refs[: count[0]], *refs[count[0] + len(after) :])

    def wrapped(*args):
        count[0] = len(args)
        return pl.pallas_call(
            skipping,
            out_shape=[jax.ShapeDtypeStruct(s, d) for s, d in outs],
            in_specs=([VMEM] * len(args) if specs is None else specs) + [ANY] * len(after),
            out_specs=[VMEM] * len(outs) if out_specs is None else out_specs,
            scratch_shapes=list(scratch),
            compiler_params=pltpu.CompilerParams(vmem_limit_bytes=limit * MIB),
            cost_estimate=pl.CostEstimate(flops=cost, bytes_accessed=0, transcendentals=0),
        )(*args, *after)

    return wrapped


BLOCKS = 4


def project_body(first, heads, order, peer, tokens, gain, send, w_qk, w_value, *rest):
    outs, (held, weights, token_sems, sems) = rest[:-4], rest[-4:]
    rows = held.shape[0]
    block = rows // BLOCKS
    loads = []
    for i in range(BLOCKS):
        part = pl.ds(i * block, block)
        loads.append(pltpu.make_async_copy(tokens.at[part], held.at[part], token_sems.at[i]))
        loads[-1].start()
    copies = []
    for h in range(heads):
        cols = pl.ds((first + h) * HEAD_DIM, HEAD_DIM)
        for j, source in enumerate((w_qk, w_value)):
            copy = pltpu.make_async_copy(
                source.at[:, cols],
                weights.at[h, :, pl.ds(j * HEAD_DIM, HEAD_DIM)],
                sems.at[2 * h + j],
            )
            copy.start()
            copies.append(copy)
    columns = to_columns(ordered_table(send[...], order, peer))
    normed = []
    for i in range(BLOCKS):
        loads[i].wait()
        floats = held[i * block : (i + 1) * block].astype(F32)
        stat = jnp.sum(floats * floats, -1, keepdims=True) * (1.0 / floats.shape[1]) + 1e-06
        normed.append((floats * lax.rsqrt(stat) * gain[...]).astype(BF16))
    normed = jnp.concatenate(normed, 0)
    for h in range(heads):
        copies[2 * h].wait()
        copies[2 * h + 1].wait()
        both = dot(normed, weights[h]).astype(BF16)
        moved = dot(by_column(columns[:, first + h : first + h + 1], rows), both).astype(BF16)
        store_rows(outs, moved, h, order, peer)


def store_rows(outs, moved, h, order, peer):
    rows = moved.shape[0]
    if order:
        part = rows // len(outs)
        for r, out in enumerate(outs):
            out[h] = moved[r * part : (r + 1) * part]
    elif peer % 16:
        outs[0][h] = moved
    else:
        for d in range(rows // peer):
            outs[0][d, h * peer : (h + 1) * peer] = moved[d * peer : (d + 1) * peer]


def row_outs(rows, heads, width, order, peer):
    if order:
        pieces = lax.axis_size("s" + order)
        return [((heads, rows // pieces, width), BF16)] * pieces
    if peer % 16:
        return [((heads, rows, width), BF16)]
    return [((rows // peer, heads * peer, width), BF16)]


def project(tokens, gain, send, w_qk, w_value, first, heads, order, peer, after=()):
    rows, depth = tokens.shape
    return call(
        functools.partial(project_body, first, heads, order, peer),
        row_outs(rows, heads, WIDTH, order, peer),
        scratch=[
            pltpu.VMEM((rows, depth), BF16),
            pltpu.VMEM((heads, depth, WIDTH), BF16),
            pltpu.SemaphoreType.DMA((BLOCKS,)),
            pltpu.SemaphoreType.DMA((2 * heads,)),
        ],
        specs=[HBM, VMEM, VMEM, HBM, HBM],
        limit=63,
        after=after,
    )(tokens, gain.reshape(1, depth), send, w_qk, w_value)


def arrived_rows(pieces, h, heads):
    if len(pieces) == 1 and pieces[0].shape[0] != heads:
        peer = pieces[0].shape[1] // heads
        own = slice(h * peer, (h + 1) * peer)
        return jnp.concatenate([pieces[0][d, own] for d in range(pieces[0].shape[0])], 0)
    return jnp.concatenate([p[h] for p in pieces], 0)


def ordered_table(table, order, peer):
    if order:
        table = relative(table, peer)
    return axes_swapped(table, "sx", peer) if order == "x" else table


def edge_body(first, order, peer, *refs):
    place, pieces, out = refs[0], refs[1:-1], refs[-1]
    rows = place.shape[1]
    index = ordered_table(axes_swapped(place[...], "sy", peer), order, peer)
    for h in range(out.shape[0]):
        table = by_row(index[first + h : first + h + 1, :], rows - SPAN, SPAN)
        out[h] = dot(table, arrived_rows(pieces, h, out.shape[0])).astype(BF16)


def unit_keys(shared):
    keys = shared.astype(F32)
    stat = jnp.sum(keys * keys, -1, keepdims=True) + 1e-06
    return (keys * lax.rsqrt(stat)).astype(BF16)


def one_span(query, unit, values):
    scores = lax.dot_general(query, unit, (((1,), (1,)), ((), ())), preferred_element_type=F32)
    scores = scores * HEAD_DIM ** (-0.5)
    rows = lax.broadcasted_iota(jnp.int32, scores.shape, 0)
    cols = lax.broadcasted_iota(jnp.int32, scores.shape, 1)
    scores = jnp.where(cols == rows + SPAN, -100000.0, scores)
    powers = jnp.exp(scores - jnp.max(scores, -1, keepdims=True))
    weights = (powers * (1.0 / jnp.sum(powers, -1, keepdims=True))).astype(BF16)
    return dot(weights, values).astype(BF16)


def inner_body(first, order, peer, *refs):
    place, edge, pieces, (head_span, out) = refs[0], refs[1], refs[2:-2], refs[-2:]
    rows = place.shape[1]
    index = ordered_table(axes_swapped(place[...], "sy", peer), order, peer)
    for h in range(out.shape[0]):
        table = by_row(index[first + h : first + h + 1, :], 0, rows - SPAN)
        ordered = dot(table, arrived_rows(pieces, h, out.shape[0])).astype(BF16)
        head_span[h] = ordered[:SPAN]
        ordered = jnp.concatenate([ordered, edge[h]], 0)
        unit = unit_keys(ordered[:, :HEAD_DIM])
        for c in range(1, rows // SPAN):
            window = slice((c - 1) * SPAN, (c + 1) * SPAN)
            out[h, (c - 1) * SPAN : c * SPAN] = one_span(
                ordered[c * SPAN : (c + 1) * SPAN, :HEAD_DIM], unit[window], ordered[window, HEAD_DIM:]
            )


def outer_body(first, order, peer, *refs):
    place, before, head_span, inner, outs = refs[0], refs[1], refs[2], refs[3], refs[4:]
    rows = place.shape[1]
    table = axes_swapped(place[...], "sy", peer)
    columns = to_columns(ordered_table(table, order, peer))
    for h in range(inner.shape[0]):
        window = jnp.concatenate([before[h], head_span[h]], 0)
        unit = unit_keys(window[:, :HEAD_DIM])
        attended = one_span(head_span[h, :, :HEAD_DIM], unit, window[:, HEAD_DIM:])
        attended = jnp.concatenate([attended, inner[h]], 0)
        moved = dot(by_column(columns[:, first + h : first + h + 1], rows), attended).astype(BF16)
        store_rows(outs, moved, h, order, peer)


def worker(block):
    n_sx, n_sy = lax.axis_size("sx"), lax.axis_size("sy")
    return block % n_sx * n_sy + block // n_sx


def attention(place, arrived, arrived_order, first, heads, order, peer, cost, after=()):
    rows = place.shape[1]
    (edge,) = call(
        functools.partial(edge_body, first, arrived_order, peer),
        [((heads, SPAN, WIDTH), BF16)],
        cost=cost,
        after=after,
    )(place, *arrived)
    peers = lax.axis_size(AXES)
    before = lax.ppermute(edge, AXES, [(worker(d), worker((d + 1) % peers)) for d in range(peers)])
    head_span, inner = call(
        functools.partial(inner_body, first, arrived_order, peer),
        [((heads, SPAN, WIDTH), BF16), ((heads, rows - SPAN, HEAD_DIM), BF16)],
        cost=cost,
    )(place, edge, *arrived)
    return call(
        functools.partial(outer_body, first, order, peer),
        row_outs(rows, heads, HEAD_DIM, order, peer),
        cost=cost,
    )(place, before, head_span, inner)


def merge_body(first, heads, order, peer, n_pieces, send, w_out, *rest):
    pieces, total, (out, weights, weight_sem) = rest[:n_pieces], rest[n_pieces:-3], rest[-3:]
    width = heads * HEAD_DIM
    load = pltpu.make_async_copy(w_out.at[pl.ds(first * HEAD_DIM, width)], weights, weight_sem)
    load.start()
    rows = send.shape[1]
    index = ordered_table(send[...], order, peer)
    merged = []
    for h in range(heads):
        table = by_row(index[first + h : first + h + 1, :], 0, rows)
        merged.append(dot(table, arrived_rows(pieces, h, heads)).astype(BF16))
    merged = jnp.concatenate(merged, 1)
    load.wait()
    result = dot(merged, weights[...])
    if total:
        result = result + total[0][...]
    out[...] = result.astype(out.dtype)


def merge(send, w_out, total, pieces, first, heads, order, peer, cost, after=()):
    rows, depth = send.shape[1], w_out.shape[1]
    width = heads * HEAD_DIM
    extra = [] if total is None else [total]
    (out,) = call(
        functools.partial(merge_body, first, heads, order, peer, len(pieces)),
        [((rows, depth), BF16)],
        scratch=[pltpu.VMEM((width, depth), BF16), pltpu.SemaphoreType.DMA(())],
        specs=[VMEM, HBM] + [VMEM] * (len(pieces) + len(extra)),
        cost=cost,
        after=after,
    )(send, w_out, *pieces, *extra)
    return out


def regroup_body(peer, *refs):
    outs = refs[-(refs[0].shape[1] // peer) :]
    pieces = refs[: -len(outs)]
    for b, out in enumerate(outs):
        for a, piece in enumerate(pieces):
            out[:, a * peer : (a + 1) * peer] = piece[:, b * peer : (b + 1) * peer]


def regroup(pieces, peer, cost, after=()):
    heads, rows, width = pieces[0].shape
    outer = rows // peer
    if peer % 16:
        table = jnp.stack(pieces, 1).reshape(heads, len(pieces), outer, peer, width)
        return [table[:, :, b].reshape(heads, -1, width) for b in range(outer)]
    return call(
        functools.partial(regroup_body, peer),
        [((heads, len(pieces) * peer, width), BF16)] * outer,
        cost=cost,
        after=after,
    )(*pieces)


def swap(array, axis, by):
    if by == 0:
        return array
    return lax.ppermute(array, axis, [(i, i ^ by) for i in range(lax.axis_size(axis))])


def exchange(pieces, axis):
    out = {r: swap(pieces[r], axis, r) for r in reversed(range(len(pieces)))}
    return [out[r] for r in range(len(pieces))]


def all_exchange(rows, tok_rows):
    devices = lax.axis_size(AXES)
    if rows.shape[1] != tok_rows:
        return lax.all_to_all(rows, BLOCKS_ALONG, split_axis=0, concat_axis=0, tiled=True)
    split = rows.reshape(rows.shape[0], devices, tok_rows // devices, rows.shape[2])
    return lax.all_to_all(split, BLOCKS_ALONG, split_axis=1, concat_axis=1, tiled=True).reshape(rows.shape)


def per_device(tokens, norm_gain, w_qk, w_value, w_out, send_order, place):
    tok_rows = tokens.shape[0]
    n_sx, n_sy = lax.axis_size("sx"), lax.axis_size("sy")
    peer = tok_rows // (n_sx * n_sy)
    place = lax.ppermute(place, AXES, [(d, worker(d)) for d in range(n_sx * n_sy)])
    (leaving,) = project(tokens, norm_gain, send_order, w_qk, w_value, 0, HEADS, "", peer)
    arrived = all_exchange(leaving, tok_rows)
    (back,) = attention(place, [arrived], "", 0, HEADS, "", peer, 0)
    returned = all_exchange(back, tok_rows)
    return merge(send_order, w_out, None, [returned], 0, HEADS, "", peer, 0)


def solution(mesh):
    return jax.shard_map(
        per_device,
        mesh=mesh,
        in_specs=(
            P(AXES, None),
            P(),
            P(),
            P(),
            P(),
            P(None, AXES),
            P(None, AXES),
        ),
        out_specs=P(AXES, None),
        check_vma=False,
    )
```

```python
import functools

import jax
import jax.numpy as jnp
from jax import lax
from jax.experimental import pallas as pl
from jax.experimental.pallas import tpu as pltpu
from jax.sharding import PartitionSpec as P

HEADS = 8
HEAD_DIM = 128
SPAN = 128
WIDTH = 2 * HEAD_DIM
AXES = ("sx", "sy")
MIB = 1024 * 1024
PARTS = 4
BF16 = jnp.bfloat16
F32 = jnp.float32
ANY = pl.BlockSpec(memory_space=pl.ANY)
HBM = pl.BlockSpec(memory_space=pltpu.HBM)
VMEM = pl.BlockSpec(memory_space=pltpu.VMEM)


def dot(a, b):
    return jnp.dot(a, b, preferred_element_type=F32)


def dot_first(a, b):
    return lax.dot_general(a, b, (((0,), (0,)), ((), ())), preferred_element_type=F32)


def dot_last(a, b):
    return lax.dot_general(a, b, (((1,), (1,)), ((), ())), preferred_element_type=F32)


def one_hot(row, first, size):
    sublanes = lax.broadcasted_iota(jnp.int32, (size, row.shape[1]), 0) + first
    return jnp.where(sublanes == row, 1.0, 0.0).astype(BF16)


def call(body, outs, scratch=(), specs=None, out_specs=None, limit=40, cost=0, after=()):
    count = [0]

    def skipping(*refs):
        return body(*refs[: count[0]], *refs[count[0] + len(after) :])

    def wrapped(*args):
        count[0] = len(args)
        return pl.pallas_call(
            skipping,
            out_shape=[jax.ShapeDtypeStruct(s, d) for s, d in outs],
            in_specs=([VMEM] * len(args) if specs is None else specs) + [ANY] * len(after),
            out_specs=[VMEM] * len(outs) if out_specs is None else out_specs,
            scratch_shapes=list(scratch),
            compiler_params=pltpu.CompilerParams(vmem_limit_bytes=limit * MIB),
            cost_estimate=pl.CostEstimate(flops=cost, bytes_accessed=0, transcendentals=0),
        )(*args, *after)

    return wrapped


def block_rows(arrived, b, peer):
    if peer % 16:
        return arrived[b]
    own = slice(b * peer, (b + 1) * peer)
    return jnp.concatenate([arrived[s, own] for s in range(arrived.shape[0])], 0)


def place_of(place, block):
    me = lax.axis_index("sx") * lax.axis_size("sy") + lax.axis_index("sy")
    return place[pl.ds((me & (HEADS - 1)) ^ block, 1), :]


def project_body(tokens, gain, send, w_qk, w_value, out, *scratch):
    held, normed, by_head, moved, wq, wv, token_sems, sems, out_sems = scratch
    rows, depth = held.shape
    block = rows // PARTS
    loads = []
    for i in range(PARTS):
        part = pl.ds(i * block, block)
        loads.append(pltpu.make_async_copy(tokens.at[part], held.at[part], token_sems.at[i]))
        loads[-1].start()
    copies = []
    for j, (source, target) in enumerate(((w_qk, wq), (w_value, wv))):
        for i in range(2):
            cols = pl.ds(i * depth // 2, depth // 2)
            copies.append(
                pltpu.make_async_copy(source.at[:, cols], target.at[:, cols], sems.at[2 * j + i])
            )
    for i in (0, 2, 1, 3):
        copies[i].start()
    for i in range(PARTS):
        loads[i].wait()
        part = slice(i * block, (i + 1) * block)
        floats = held[part].astype(F32)
        stat = jnp.sum(floats * floats, -1, keepdims=True) * (1.0 / depth) + 1e-06
        normed[part] = (floats * lax.rsqrt(stat) * gain[...]).astype(BF16)
    for p in range(HEADS // 2):
        if p % (HEADS // 4) == 0:
            i = p // (HEADS // 4)
            copies[i].wait()
            copies[2 + i].wait()
        cols = slice(p * WIDTH, (p + 1) * WIDTH)
        for j, weights in enumerate((wq, wv)):
            both = dot(normed[...], weights[:, cols]).astype(BF16)
            side = slice(j * HEAD_DIM, (j + 1) * HEAD_DIM)
            by_head[2 * p, :, side] = both[:, :HEAD_DIM]
            by_head[2 * p + 1, :, side] = both[:, HEAD_DIM:]
    stores = []
    runs, size = moved.shape[1], moved.shape[2]
    for h in range(HEADS):
        table = one_hot(send[h : h + 1, :], 0, rows)
        rows_of_head = dot_first(table, by_head[h]).astype(BF16)
        for g in range(runs):
            moved[h, g] = rows_of_head[g * size : (g + 1) * size]
        stores.append(pltpu.make_async_copy(moved.at[h], out.at[:, h], out_sems.at[h]))
        stores[-1].start()
    for store in stores:
        store.wait()


def edge_body(peer, place, arrived, out):
    rows = place.shape[1]
    table = one_hot(place_of(place, HEADS - 1), rows - SPAN, SPAN)
    out[...] = dot(table, block_rows(arrived, HEADS - 1, peer)).astype(BF16)


def unit_keys(shared):
    keys = shared.astype(F32)
    stat = jnp.sum(keys * keys, -1, keepdims=True) + 1e-06
    return (keys * lax.rsqrt(stat)).astype(BF16)


def one_span(query, unit, values):
    root = HEAD_DIM**0.5
    scores = dot_last(unit, query)
    keys = lax.broadcasted_iota(jnp.int32, scores.shape, 0)
    queries = lax.broadcasted_iota(jnp.int32, scores.shape, 1)
    scores = jnp.where(keys == queries + SPAN, -100000.0 * root, scores)
    shifted = scores - jnp.max(scores, 0, keepdims=True)
    powers = jnp.exp2(shifted * (1.4426950408889634 / root))
    weights = (powers * (1.0 / jnp.sum(powers, 0, keepdims=True))).astype(BF16)
    return dot_first(weights, values).astype(BF16)


def store_block(out, moved, b, peer):
    if peer % 16:
        out[b] = moved
        return
    for s in range(out.shape[0]):
        out[s, b * peer : (b + 1) * peer] = moved[s * peer : (s + 1) * peer]


def inner_body(peer, place, arrived, head_span, first_block, leaving, ordered, unit, attended):
    rows = place.shape[1]
    for b in range(HEADS):
        table = one_hot(place_of(place, b), 0, rows)
        ordered[b * rows : (b + 1) * rows] = dot(table, block_rows(arrived, b, peer)).astype(BF16)
    for b in range(HEADS):
        part = slice(b * rows, (b + 1) * rows)
        unit[part] = unit_keys(ordered[part, :HEAD_DIM])
    head_span[...] = ordered[:SPAN]
    attended[:SPAN] = jnp.zeros((SPAN, HEAD_DIM), BF16)
    for c in range(1, HEADS * rows // SPAN):
        own = slice(c * SPAN, (c + 1) * SPAN)
        window = slice((c - 1) * SPAN, (c + 1) * SPAN)
        attended[own] = one_span(ordered[own, :HEAD_DIM], unit[window], ordered[window, HEAD_DIM:])
    for b in range(HEADS):
        table = one_hot(place_of(place, b), 0, rows)
        moved = dot_first(table, attended[b * rows : (b + 1) * rows]).astype(BF16)
        if b:
            store_block(leaving, moved, b, peer)
        else:
            first_block[...] = moved


def outer_body(peer, place, before, head_span, first_block, leaving, out, window, unit, attended):
    window[:SPAN] = before[...]
    window[SPAN:] = head_span[...]
    unit[...] = unit_keys(window[:, :HEAD_DIM])
    attended[...] = one_span(head_span[:, :HEAD_DIM], unit[...], window[:, HEAD_DIM:])
    moved = dot_first(one_hot(place_of(place, 0), 0, SPAN), attended[...]).astype(BF16)
    store_block(out, first_block[...] + moved, 0, peer)
    if peer % 16:
        out[1:] = leaving[1:]
    else:
        out[:, peer:] = leaving[:, peer:]


def merge_body(send, arrived, w_out, out, merged, result, sems):
    rows = send.shape[1]
    runs = arrived.shape[0] // HEADS
    for h in range(HEADS):
        table = one_hot(send[h : h + 1, :], 0, rows)
        cols = slice(h * HEAD_DIM, (h + 1) * HEAD_DIM)
        rows_of_head = jnp.concatenate([arrived[g * HEADS + h] for g in range(runs)], 0)
        merged[:, cols] = dot(table, rows_of_head).astype(BF16)
    block = rows // PARTS
    copies = []
    for i in range(PARTS):
        part = slice(i * block, (i + 1) * block)
        result[part] = dot(merged[part], w_out[...]).astype(BF16)
        copies.append(
            pltpu.make_async_copy(
                result.at[pl.ds(i * block, block)], out.at[pl.ds(i * block, block)], sems.at[i]
            )
        )
        copies[-1].start()
    for copy in copies:
        copy.wait()


def by_block(rows, peer):
    if peer % 16 == 0:
        return rows
    devices, size, width = rows.shape
    split = rows.reshape(devices, size // peer, peer, width).transpose(1, 0, 2, 3)
    return split.reshape(size // peer, devices * peer, width)


def by_device(rows, peer):
    if peer % 16 == 0:
        return rows
    blocks, size, width = rows.shape
    split = rows.reshape(blocks, size // peer, peer, width).transpose(1, 0, 2, 3)
    return split.reshape(size // peer, blocks * peer, width)


def exchange(rows):
    return lax.all_to_all(rows, AXES, split_axis=0, concat_axis=0, tiled=True)


def per_device(tokens, norm_gain, w_qk, w_value, w_out, send_order, place):
    rows, depth = tokens.shape
    devices = lax.axis_size(AXES)
    peer = rows // devices
    runs = devices // HEADS
    me = lax.axis_index(AXES) % HEADS

    def turned(table, bit):
        split = table.reshape(HEADS // (2 * bit), 2, bit, rows)
        return jnp.where((me & bit) > 0, jnp.flip(split, 1), split).reshape(HEADS, rows)

    def traded(table, by):
        return lax.ppermute(table, AXES, [(i, i ^ by) for i in range(devices)])

    half = HEADS // 2
    place = turned(place, half)
    near, far = place[:half], traded(place[half:], half)
    place = jnp.concatenate([near, far], 0)
    bit = 1
    while bit < half:
        place = turned(place, bit)
        bit *= 2
    place = place.reshape(2, half, rows)
    parts = [traded(place[:, r], r) if r else place[:, r] for r in range(half)]
    place = jnp.stack(parts, 1).reshape(HEADS, rows)

    (leaving,) = call(
        project_body,
        [((runs, HEADS, rows // runs, WIDTH), BF16)],
        scratch=[
            pltpu.VMEM((rows, depth), BF16),
            pltpu.VMEM((rows, depth), BF16),
            pltpu.VMEM((HEADS, rows, WIDTH), BF16),
            pltpu.VMEM((HEADS, runs, rows // runs, WIDTH), BF16),
            pltpu.VMEM(w_qk.shape, BF16),
            pltpu.VMEM(w_value.shape, BF16),
            pltpu.SemaphoreType.DMA((PARTS,)),
            pltpu.SemaphoreType.DMA((4,)),
            pltpu.SemaphoreType.DMA((HEADS,)),
        ],
        specs=[HBM, VMEM, VMEM, HBM, HBM],
        out_specs=[HBM],
        limit=60,
        cost=2 * rows * HEADS * WIDTH * (depth + rows),
    )(tokens, norm_gain.reshape(1, depth), send_order, w_qk, w_value)
    arrived = exchange(leaving.reshape(devices, rows // runs, WIDTH))
    arrived = by_block(arrived, peer)
    (edge,) = call(functools.partial(edge_body, peer), [((SPAN, WIDTH), BF16)])(place, arrived)
    onward = [(i, (i + HEADS) % devices) for i in range(devices)]
    before = lax.ppermute(edge, AXES, onward)
    gone = (HEADS, rows, HEAD_DIM) if peer % 16 else (devices, HEADS * peer, HEAD_DIM)
    head_span, first_block, partly = call(
        functools.partial(inner_body, peer),
        [((SPAN, WIDTH), BF16), ((rows, HEAD_DIM), BF16), (gone, BF16)],
        scratch=[
            pltpu.VMEM((HEADS * rows, WIDTH), BF16),
            pltpu.VMEM((HEADS * rows, HEAD_DIM), BF16),
            pltpu.VMEM((HEADS * rows, HEAD_DIM), BF16),
        ],
        after=[edge],
    )(place, arrived)
    (back,) = call(
        functools.partial(outer_body, peer),
        [(gone, BF16)],
        scratch=[
            pltpu.VMEM((2 * SPAN, WIDTH), BF16),
            pltpu.VMEM((2 * SPAN, HEAD_DIM), BF16),
            pltpu.VMEM((SPAN, HEAD_DIM), BF16),
        ],
    )(place, before, head_span, first_block, partly)
    returned = exchange(by_device(back, peer))
    (out,) = call(
        merge_body,
        [((rows, w_out.shape[1]), BF16)],
        scratch=[
            pltpu.VMEM((rows, HEADS * HEAD_DIM), BF16),
            pltpu.VMEM((rows, w_out.shape[1]), BF16),
            pltpu.SemaphoreType.DMA((PARTS,)),
        ],
        out_specs=[HBM],
        limit=20,
    )(send_order, returned, w_out)
    return out


def solution(mesh):
    return jax.shard_map(
        per_device,
        mesh=mesh,
        in_specs=(
            P(AXES, None),
            P(),
            P(),
            P(),
            P(),
            P(None, AXES),
            P(None, AXES),
        ),
        out_specs=P(AXES, None),
        check_vma=False,
    )
```

```python
import functools

import jax
import jax.numpy as jnp
from jax import lax
from jax.experimental import pallas as pl
from jax.experimental.pallas import tpu as pltpu
from jax.sharding import PartitionSpec as P

HEADS = 8
HEAD_DIM = 128
SPAN = 128
WIDTH = 2 * HEAD_DIM
AXES = ("sx", "sy")
MIB = 1024 * 1024
PARTS = 4
BF16 = jnp.bfloat16
F32 = jnp.float32
ANY = pl.BlockSpec(memory_space=pl.ANY)
HBM = pl.BlockSpec(memory_space=pltpu.HBM)
VMEM = pl.BlockSpec(memory_space=pltpu.VMEM)


def dot(a, b):
    return jnp.dot(a, b, preferred_element_type=F32)


def dot_first(a, b):
    return lax.dot_general(a, b, (((0,), (0,)), ((), ())), preferred_element_type=F32)


def dot_last(a, b):
    return lax.dot_general(a, b, (((1,), (1,)), ((), ())), preferred_element_type=F32)


def one_hot(row, first, size):
    sublanes = lax.broadcasted_iota(jnp.int32, (size, row.shape[1]), 0) + first
    return jnp.where(sublanes == row, 1.0, 0.0).astype(BF16)


def call(body, outs, scratch=(), specs=None, out_specs=None, limit=40, cost=0, after=()):
    count = [0]

    def skipping(*refs):
        return body(*refs[: count[0]], *refs[count[0] + len(after) :])

    def wrapped(*args):
        count[0] = len(args)
        return pl.pallas_call(
            skipping,
            out_shape=[jax.ShapeDtypeStruct(s, d) for s, d in outs],
            in_specs=([VMEM] * len(args) if specs is None else specs) + [ANY] * len(after),
            out_specs=[VMEM] * len(outs) if out_specs is None else out_specs,
            scratch_shapes=list(scratch),
            compiler_params=pltpu.CompilerParams(vmem_limit_bytes=limit * MIB),
            cost_estimate=pl.CostEstimate(flops=cost, bytes_accessed=0, transcendentals=0),
        )(*args, *after)

    return wrapped


def block_rows(arrived, b, peer):
    if peer % 16:
        return arrived[b]
    own = slice(b * peer, (b + 1) * peer)
    return jnp.concatenate([arrived[s, own] for s in range(arrived.shape[0])], 0)


def place_of(place, block):
    me = lax.axis_index("sx") * lax.axis_size("sy") + lax.axis_index("sy")
    return place[pl.ds((me & (HEADS - 1)) ^ block, 1), :]


def project_body(tokens, gain, send, w_qk, w_value, out, *scratch):
    held, normed, by_head, moved, wq, wv, token_sems, sems, out_sems = scratch
    rows, depth = held.shape
    block = rows // PARTS
    loads = []
    for i in range(PARTS):
        part = pl.ds(i * block, block)
        loads.append(pltpu.make_async_copy(tokens.at[part], held.at[part], token_sems.at[i]))
        loads[-1].start()
    copies = []
    for j, (source, target) in enumerate(((w_qk, wq), (w_value, wv))):
        for i in range(2):
            cols = pl.ds(i * depth // 2, depth // 2)
            copies.append(
                pltpu.make_async_copy(source.at[:, cols], target.at[:, cols], sems.at[2 * j + i])
            )
    for i in (0, 2, 1, 3):
        copies[i].start()
    def norm(i):
        loads[i].wait()
        norm_rest(i)

    def norm_rest(i):
        part = slice(i * block, (i + 1) * block)
        floats = held[part].astype(F32)
        stat = jnp.sum(floats * floats, -1, keepdims=True) * (1.0 / depth) + 1e-06
        normed[part] = (floats * lax.rsqrt(stat) * gain[...]).astype(BF16)

    def multiply(part, pairs):
        for p in pairs:
            cols = slice(p * WIDTH, (p + 1) * WIDTH)
            for j, weights in enumerate((wq, wv)):
                both = dot(normed[part], weights[:, cols]).astype(BF16)
                side = slice(j * HEAD_DIM, (j + 1) * HEAD_DIM)
                by_head[2 * p, part, side] = both[:, :HEAD_DIM]
                by_head[2 * p + 1, part, side] = both[:, HEAD_DIM:]

    early, late = range(HEADS // 4), range(HEADS // 4, HEADS // 2)
    top, bottom = slice(0, rows // 2), slice(rows // 2, rows)
    for i in range(PARTS // 2):
        norm(i)
    copies[0].wait()
    copies[2].wait()
    for i in range(PARTS // 2, PARTS):
        loads[i].wait()
    multiply(top, early)
    for i in range(PARTS // 2, PARTS):
        norm_rest(i)
    multiply(bottom, early)
    copies[1].wait()
    copies[3].wait()
    multiply(slice(0, rows), late)
    stores = []
    runs, size = moved.shape[1], moved.shape[2]
    for h in range(HEADS):
        table = one_hot(send[h : h + 1, :], 0, rows)
        rows_of_head = dot_first(table, by_head[h]).astype(BF16)
        for g in range(runs):
            moved[h, g] = rows_of_head[g * size : (g + 1) * size]
        stores.append(pltpu.make_async_copy(moved.at[h], out.at[:, h], out_sems.at[h]))
        stores[-1].start()
    for store in stores:
        store.wait()


def edge_body(peer, place, arrived, out):
    rows = place.shape[1]
    table = one_hot(place_of(place, HEADS - 1), rows - SPAN, SPAN)
    out[...] = dot(table, block_rows(arrived, HEADS - 1, peer)).astype(BF16)


def unit_keys(shared):
    keys = shared.astype(F32)
    stat = jnp.sum(keys * keys, -1, keepdims=True) + 1e-06
    return (keys * lax.rsqrt(stat)).astype(BF16)


def one_span(query, unit, values):
    root = HEAD_DIM**0.5
    scores = dot_last(unit, query)
    keys = lax.broadcasted_iota(jnp.int32, scores.shape, 0)
    queries = lax.broadcasted_iota(jnp.int32, scores.shape, 1)
    scores = jnp.where(keys == queries + SPAN, -100000.0 * root, scores)
    shifted = scores - jnp.max(scores, 0, keepdims=True)
    powers = jnp.exp2(shifted * (1.4426950408889634 / root))
    weights = (powers * (1.0 / jnp.sum(powers, 0, keepdims=True))).astype(BF16)
    return dot_first(weights, values).astype(BF16)


def store_block(out, moved, b, peer):
    if peer % 16:
        out[b] = moved
        return
    for s in range(out.shape[0]):
        out[s, b * peer : (b + 1) * peer] = moved[s * peer : (s + 1) * peer]


def inner_body(peer, place, arrived, head_span, first_block, leaving, ordered, unit, attended):
    rows = place.shape[1]
    for b in range(HEADS):
        table = one_hot(place_of(place, b), 0, rows)
        ordered[b * rows : (b + 1) * rows] = dot(table, block_rows(arrived, b, peer)).astype(BF16)
    for b in range(HEADS):
        part = slice(b * rows, (b + 1) * rows)
        unit[part] = unit_keys(ordered[part, :HEAD_DIM])
    head_span[...] = ordered[:SPAN]
    attended[:SPAN] = jnp.zeros((SPAN, HEAD_DIM), BF16)
    for c in range(1, HEADS * rows // SPAN):
        own = slice(c * SPAN, (c + 1) * SPAN)
        window = slice((c - 1) * SPAN, (c + 1) * SPAN)
        attended[own] = one_span(ordered[own, :HEAD_DIM], unit[window], ordered[window, HEAD_DIM:])
    for b in range(HEADS):
        table = one_hot(place_of(place, b), 0, rows)
        moved = dot_first(table, attended[b * rows : (b + 1) * rows]).astype(BF16)
        if b:
            store_block(leaving, moved, b, peer)
        else:
            first_block[...] = moved


def outer_body(peer, place, before, head_span, first_block, leaving, out, window, unit, attended):
    window[:SPAN] = before[...]
    window[SPAN:] = head_span[...]
    unit[...] = unit_keys(window[:, :HEAD_DIM])
    attended[...] = one_span(head_span[:, :HEAD_DIM], unit[...], window[:, HEAD_DIM:])
    moved = dot_first(one_hot(place_of(place, 0), 0, SPAN), attended[...]).astype(BF16)
    store_block(out, first_block[...] + moved, 0, peer)
    if peer % 16:
        out[1:] = leaving[1:]
    else:
        out[:, peer:] = leaving[:, peer:]


def merge_body(send, arrived, w_out, out, merged, result, sems):
    rows = send.shape[1]
    runs = arrived.shape[0] // HEADS
    for h in range(HEADS):
        table = one_hot(send[h : h + 1, :], 0, rows)
        cols = slice(h * HEAD_DIM, (h + 1) * HEAD_DIM)
        rows_of_head = jnp.concatenate([arrived[g * HEADS + h] for g in range(runs)], 0)
        merged[:, cols] = dot(table, rows_of_head).astype(BF16)
    block = rows // PARTS
    copies = []
    for i in range(PARTS):
        part = slice(i * block, (i + 1) * block)
        result[part] = dot(merged[part], w_out[...]).astype(BF16)
        copies.append(
            pltpu.make_async_copy(
                result.at[pl.ds(i * block, block)], out.at[pl.ds(i * block, block)], sems.at[i]
            )
        )
        copies[-1].start()
    for copy in copies:
        copy.wait()


def by_block(rows, peer):
    if peer % 16 == 0:
        return rows
    devices, size, width = rows.shape
    split = rows.reshape(devices, size // peer, peer, width).transpose(1, 0, 2, 3)
    return split.reshape(size // peer, devices * peer, width)


def by_device(rows, peer):
    if peer % 16 == 0:
        return rows
    blocks, size, width = rows.shape
    split = rows.reshape(blocks, size // peer, peer, width).transpose(1, 0, 2, 3)
    return split.reshape(size // peer, blocks * peer, width)


def exchange(rows):
    return lax.all_to_all(rows, AXES, split_axis=0, concat_axis=0, tiled=True)


def per_device(tokens, norm_gain, w_qk, w_value, w_out, send_order, place):
    rows, depth = tokens.shape
    devices = lax.axis_size(AXES)
    peer = rows // devices
    runs = devices // HEADS
    me = lax.axis_index(AXES) % HEADS

    def turned(table, bit):
        split = table.reshape(HEADS // (2 * bit), 2, bit, rows)
        return jnp.where((me & bit) > 0, jnp.flip(split, 1), split).reshape(HEADS, rows)

    def traded(table, by):
        return lax.ppermute(table, AXES, [(i, i ^ by) for i in range(devices)])

    half = HEADS // 2
    place = turned(place, half)
    near, far = place[:half], traded(place[half:], half)
    place = jnp.concatenate([near, far], 0)
    bit = 1
    while bit < half:
        place = turned(place, bit)
        bit *= 2
    place = place.reshape(2, half, rows)
    parts = [traded(place[:, r], r) if r else place[:, r] for r in range(half)]
    place = jnp.stack(parts, 1).reshape(HEADS, rows)

    (leaving,) = call(
        project_body,
        [((runs, HEADS, rows // runs, WIDTH), BF16)],
        scratch=[
            pltpu.VMEM((rows, depth), BF16),
            pltpu.VMEM((rows, depth), BF16),
            pltpu.VMEM((HEADS, rows, WIDTH), BF16),
            pltpu.VMEM((HEADS, runs, rows // runs, WIDTH), BF16),
            pltpu.VMEM(w_qk.shape, BF16),
            pltpu.VMEM(w_value.shape, BF16),
            pltpu.SemaphoreType.DMA((PARTS,)),
            pltpu.SemaphoreType.DMA((4,)),
            pltpu.SemaphoreType.DMA((HEADS,)),
        ],
        specs=[HBM, VMEM, VMEM, HBM, HBM],
        out_specs=[HBM],
        limit=60,
        cost=2 * rows * HEADS * WIDTH * (depth + rows),
    )(tokens, norm_gain.reshape(1, depth), send_order, w_qk, w_value)
    arrived = exchange(leaving.reshape(devices, rows // runs, WIDTH))
    arrived = by_block(arrived, peer)
    (edge,) = call(functools.partial(edge_body, peer), [((SPAN, WIDTH), BF16)])(place, arrived)
    onward = [(i, (i + HEADS) % devices) for i in range(devices)]
    before = lax.ppermute(edge, AXES, onward)
    gone = (HEADS, rows, HEAD_DIM) if peer % 16 else (devices, HEADS * peer, HEAD_DIM)
    head_span, first_block, partly = call(
        functools.partial(inner_body, peer),
        [((SPAN, WIDTH), BF16), ((rows, HEAD_DIM), BF16), (gone, BF16)],
        scratch=[
            pltpu.VMEM((HEADS * rows, WIDTH), BF16),
            pltpu.VMEM((HEADS * rows, HEAD_DIM), BF16),
            pltpu.VMEM((HEADS * rows, HEAD_DIM), BF16),
        ],
        after=[edge],
    )(place, arrived)
    (back,) = call(
        functools.partial(outer_body, peer),
        [(gone, BF16)],
        scratch=[
            pltpu.VMEM((2 * SPAN, WIDTH), BF16),
            pltpu.VMEM((2 * SPAN, HEAD_DIM), BF16),
            pltpu.VMEM((SPAN, HEAD_DIM), BF16),
        ],
    )(place, before, head_span, first_block, partly)
    returned = exchange(by_device(back, peer))
    (out,) = call(
        merge_body,
        [((rows, w_out.shape[1]), BF16)],
        scratch=[
            pltpu.VMEM((rows, HEADS * HEAD_DIM), BF16),
            pltpu.VMEM((rows, w_out.shape[1]), BF16),
            pltpu.SemaphoreType.DMA((PARTS,)),
        ],
        out_specs=[HBM],
        limit=20,
    )(send_order, returned, w_out)
    return out


def solution(mesh):
    return jax.shard_map(
        per_device,
        mesh=mesh,
        in_specs=(
            P(AXES, None),
            P(),
            P(),
            P(),
            P(),
            P(None, AXES),
            P(None, AXES),
        ),
        out_specs=P(AXES, None),
        check_vma=False,
    )
```

```python
import functools

import jax
import jax.numpy as jnp
from jax import lax
from jax.experimental import pallas as pl
from jax.experimental.pallas import tpu as pltpu
from jax.sharding import PartitionSpec as P

HEADS = 8
HEAD_DIM = 128
SPAN = 128
WIDTH = 2 * HEAD_DIM
AXES = ("sx", "sy")
MIB = 1024 * 1024
PARTS = 4
STORES = 2
BF16 = jnp.bfloat16
F32 = jnp.float32
ANY = pl.BlockSpec(memory_space=pl.ANY)
HBM = pl.BlockSpec(memory_space=pltpu.HBM)
VMEM = pl.BlockSpec(memory_space=pltpu.VMEM)


def dot(a, b):
    return jnp.dot(a, b, preferred_element_type=F32)


def dot_first(a, b):
    return lax.dot_general(a, b, (((0,), (0,)), ((), ())), preferred_element_type=F32)


def dot_last(a, b):
    return lax.dot_general(a, b, (((1,), (1,)), ((), ())), preferred_element_type=F32)


def one_hot(row, first, size):
    sublanes = lax.broadcasted_iota(jnp.int32, (size, row.shape[1]), 0) + first
    return jnp.where(sublanes == row, 1.0, 0.0).astype(BF16)


def call(body, outs, scratch=(), specs=None, out_specs=None, limit=40, cost=0, after=()):
    count = [0]

    def skipping(*refs):
        return body(*refs[: count[0]], *refs[count[0] + len(after) :])

    def wrapped(*args):
        count[0] = len(args)
        return pl.pallas_call(
            skipping,
            out_shape=[jax.ShapeDtypeStruct(s, d) for s, d in outs],
            in_specs=([VMEM] * len(args) if specs is None else specs) + [ANY] * len(after),
            out_specs=[VMEM] * len(outs) if out_specs is None else out_specs,
            scratch_shapes=list(scratch),
            compiler_params=pltpu.CompilerParams(vmem_limit_bytes=limit * MIB),
            cost_estimate=pl.CostEstimate(flops=cost, bytes_accessed=0, transcendentals=0),
        )(*args, *after)

    return wrapped


def block_rows(arrived, b, peer):
    if peer % 16:
        return arrived[b]
    own = slice(b * peer, (b + 1) * peer)
    return jnp.concatenate([arrived[s, own] for s in range(arrived.shape[0])], 0)


def place_of(place, block):
    me = lax.axis_index("sx") * lax.axis_size("sy") + lax.axis_index("sy")
    return place[pl.ds((me & (HEADS - 1)) ^ block, 1), :]


def project_body(tokens, gain, send, w_qk, w_value, out, *scratch):
    held, normed, by_head, moved, wq, wv, token_sems, sems, out_sems = scratch
    rows, depth = held.shape
    block = rows // PARTS
    loads = []
    for i in range(PARTS):
        part = pl.ds(i * block, block)
        loads.append(pltpu.make_async_copy(tokens.at[part], held.at[part], token_sems.at[i]))
        loads[-1].start()
    copies = []
    for j, (source, target) in enumerate(((w_qk, wq), (w_value, wv))):
        for i in range(2):
            cols = pl.ds(i * depth // 2, depth // 2)
            copies.append(
                pltpu.make_async_copy(source.at[:, cols], target.at[:, cols], sems.at[2 * j + i])
            )
    for i in (0, 2, 1, 3):
        copies[i].start()
    def norm(i):
        loads[i].wait()
        norm_rest(i)

    def norm_rest(i):
        part = slice(i * block, (i + 1) * block)
        floats = held[part].astype(F32)
        stat = jnp.sum(floats * floats, -1, keepdims=True) * (1.0 / depth) + 1e-06
        normed[part] = (floats * lax.rsqrt(stat) * gain[...]).astype(BF16)

    def multiply(part, pairs):
        for p in pairs:
            cols = slice(p * WIDTH, (p + 1) * WIDTH)
            for j, weights in enumerate((wq, wv)):
                both = dot(normed[part], weights[:, cols]).astype(BF16)
                side = slice(j * HEAD_DIM, (j + 1) * HEAD_DIM)
                by_head[2 * p, part, side] = both[:, :HEAD_DIM]
                by_head[2 * p + 1, part, side] = both[:, HEAD_DIM:]

    early, late = range(HEADS // 4), range(HEADS // 4, HEADS // 2)
    top, bottom = slice(0, rows // 2), slice(rows // 2, rows)
    for i in range(PARTS // 2):
        norm(i)
    copies[0].wait()
    copies[2].wait()
    for i in range(PARTS // 2, PARTS):
        loads[i].wait()
    multiply(top, early)
    for i in range(PARTS // 2, PARTS):
        norm_rest(i)
    multiply(bottom, early)
    copies[1].wait()
    copies[3].wait()
    multiply(slice(0, rows), late)
    stores = []
    runs, size = moved.shape[1], moved.shape[2]
    for h in range(HEADS):
        table = one_hot(send[h : h + 1, :], 0, rows)
        rows_of_head = dot_first(table, by_head[h]).astype(BF16)
        for g in range(runs):
            moved[h, g] = rows_of_head[g * size : (g + 1) * size]
        stores.append(pltpu.make_async_copy(moved.at[h], out.at[:, h], out_sems.at[h]))
        stores[-1].start()
    for store in stores:
        store.wait()


def edge_body(peer, place, arrived, out):
    rows = place.shape[1]
    table = one_hot(place_of(place, HEADS - 1), rows - SPAN, SPAN)
    out[...] = dot(table, block_rows(arrived, HEADS - 1, peer)).astype(BF16)


def unit_keys(shared):
    keys = shared.astype(F32)
    stat = jnp.sum(keys * keys, -1, keepdims=True) + 1e-06
    return (keys * lax.rsqrt(stat)).astype(BF16)


def one_span(query, unit, values):
    root = HEAD_DIM**0.5
    scores = dot_last(unit, query)
    keys = lax.broadcasted_iota(jnp.int32, scores.shape, 0)
    queries = lax.broadcasted_iota(jnp.int32, scores.shape, 1)
    scores = jnp.where(keys == queries + SPAN, -100000.0 * root, scores)
    shifted = scores - jnp.max(scores, 0, keepdims=True)
    powers = jnp.exp2(shifted * (1.4426950408889634 / root))
    weights = (powers * (1.0 / jnp.sum(powers, 0, keepdims=True))).astype(BF16)
    return dot_first(weights, values).astype(BF16)


def store_block(out, moved, b, peer):
    if peer % 16:
        out[b] = moved
        return
    for s in range(out.shape[0]):
        out[s, b * peer : (b + 1) * peer] = moved[s * peer : (s + 1) * peer]


def inner_body(peer, place, arrived, head_span, first_block, leaving, ordered, unit, attended):
    rows = place.shape[1]
    for b in range(HEADS):
        table = one_hot(place_of(place, b), 0, rows)
        ordered[b * rows : (b + 1) * rows] = dot(table, block_rows(arrived, b, peer)).astype(BF16)
    for b in range(HEADS):
        part = slice(b * rows, (b + 1) * rows)
        unit[part] = unit_keys(ordered[part, :HEAD_DIM])
    head_span[...] = ordered[:SPAN]
    attended[:SPAN] = jnp.zeros((SPAN, HEAD_DIM), BF16)
    for c in range(1, HEADS * rows // SPAN):
        own = slice(c * SPAN, (c + 1) * SPAN)
        window = slice((c - 1) * SPAN, (c + 1) * SPAN)
        attended[own] = one_span(ordered[own, :HEAD_DIM], unit[window], ordered[window, HEAD_DIM:])
    for b in range(HEADS):
        table = one_hot(place_of(place, b), 0, rows)
        moved = dot_first(table, attended[b * rows : (b + 1) * rows]).astype(BF16)
        if b:
            store_block(leaving, moved, b, peer)
        else:
            first_block[...] = moved


def outer_body(peer, place, before, head_span, first_block, leaving, out, window, unit, attended):
    window[:SPAN] = before[...]
    window[SPAN:] = head_span[...]
    unit[...] = unit_keys(window[:, :HEAD_DIM])
    attended[...] = one_span(head_span[:, :HEAD_DIM], unit[...], window[:, HEAD_DIM:])
    moved = dot_first(one_hot(place_of(place, 0), 0, SPAN), attended[...]).astype(BF16)
    store_block(out, first_block[...] + moved, 0, peer)
    if peer % 16:
        out[1:] = leaving[1:]
    else:
        out[:, peer:] = leaving[:, peer:]


def merge_body(send, arrived, w_out, out, merged, result, sems):
    rows = send.shape[1]
    runs = arrived.shape[0] // HEADS
    for h in range(HEADS):
        table = one_hot(send[h : h + 1, :], 0, rows)
        cols = slice(h * HEAD_DIM, (h + 1) * HEAD_DIM)
        rows_of_head = jnp.concatenate([arrived[g * HEADS + h] for g in range(runs)], 0)
        merged[:, cols] = dot(table, rows_of_head).astype(BF16)
    block = rows // STORES
    copies = []
    for i in range(STORES):
        part = slice(i * block, (i + 1) * block)
        result[part] = dot(merged[part], w_out[...]).astype(BF16)
        copies.append(
            pltpu.make_async_copy(
                result.at[pl.ds(i * block, block)], out.at[pl.ds(i * block, block)], sems.at[i]
            )
        )
        copies[-1].start()
    for copy in copies:
        copy.wait()


def by_block(rows, peer):
    if peer % 16 == 0:
        return rows
    devices, size, width = rows.shape
    split = rows.reshape(devices, size // peer, peer, width).transpose(1, 0, 2, 3)
    return split.reshape(size // peer, devices * peer, width)


def by_device(rows, peer):
    if peer % 16 == 0:
        return rows
    blocks, size, width = rows.shape
    split = rows.reshape(blocks, size // peer, peer, width).transpose(1, 0, 2, 3)
    return split.reshape(size // peer, blocks * peer, width)


def exchange(rows):
    return lax.all_to_all(rows, AXES, split_axis=0, concat_axis=0, tiled=True)


def per_device(tokens, norm_gain, w_qk, w_value, w_out, send_order, place):
    rows, depth = tokens.shape
    devices = lax.axis_size(AXES)
    peer = rows // devices
    runs = devices // HEADS
    me = lax.axis_index(AXES) % HEADS

    def turned(table, bit):
        split = table.reshape(HEADS // (2 * bit), 2, bit, rows)
        return jnp.where((me & bit) > 0, jnp.flip(split, 1), split).reshape(HEADS, rows)

    def traded(table, by):
        return lax.ppermute(table, AXES, [(i, i ^ by) for i in range(devices)])

    half = HEADS // 2
    place = turned(place, half)
    near, far = place[:half], traded(place[half:], half)
    place = jnp.concatenate([near, far], 0)
    bit = 1
    while bit < half:
        place = turned(place, bit)
        bit *= 2
    place = place.reshape(2, half, rows)
    parts = [traded(place[:, r], r) if r else place[:, r] for r in range(half)]
    place = jnp.stack(parts, 1).reshape(HEADS, rows)

    (leaving,) = call(
        project_body,
        [((runs, HEADS, rows // runs, WIDTH), BF16)],
        scratch=[
            pltpu.VMEM((rows, depth), BF16),
            pltpu.VMEM((rows, depth), BF16),
            pltpu.VMEM((HEADS, rows, WIDTH), BF16),
            pltpu.VMEM((HEADS, runs, rows // runs, WIDTH), BF16),
            pltpu.VMEM(w_qk.shape, BF16),
            pltpu.VMEM(w_value.shape, BF16),
            pltpu.SemaphoreType.DMA((PARTS,)),
            pltpu.SemaphoreType.DMA((4,)),
            pltpu.SemaphoreType.DMA((HEADS,)),
        ],
        specs=[HBM, VMEM, VMEM, HBM, HBM],
        out_specs=[HBM],
        limit=60,
        cost=2 * rows * HEADS * WIDTH * (depth + rows),
    )(tokens, norm_gain.reshape(1, depth), send_order, w_qk, w_value)
    arrived = exchange(leaving.reshape(devices, rows // runs, WIDTH))
    arrived = by_block(arrived, peer)
    (edge,) = call(functools.partial(edge_body, peer), [((SPAN, WIDTH), BF16)])(place, arrived)
    onward = [(i, (i + HEADS) % devices) for i in range(devices)]
    before = lax.ppermute(edge, AXES, onward)
    gone = (HEADS, rows, HEAD_DIM) if peer % 16 else (devices, HEADS * peer, HEAD_DIM)
    head_span, first_block, partly = call(
        functools.partial(inner_body, peer),
        [((SPAN, WIDTH), BF16), ((rows, HEAD_DIM), BF16), (gone, BF16)],
        scratch=[
            pltpu.VMEM((HEADS * rows, WIDTH), BF16),
            pltpu.VMEM((HEADS * rows, HEAD_DIM), BF16),
            pltpu.VMEM((HEADS * rows, HEAD_DIM), BF16),
        ],
        after=[edge],
    )(place, arrived)
    (back,) = call(
        functools.partial(outer_body, peer),
        [(gone, BF16)],
        scratch=[
            pltpu.VMEM((2 * SPAN, WIDTH), BF16),
            pltpu.VMEM((2 * SPAN, HEAD_DIM), BF16),
            pltpu.VMEM((SPAN, HEAD_DIM), BF16),
        ],
    )(place, before, head_span, first_block, partly)
    returned = exchange(by_device(back, peer))
    (out,) = call(
        merge_body,
        [((rows, w_out.shape[1]), BF16)],
        scratch=[
            pltpu.VMEM((rows, HEADS * HEAD_DIM), BF16),
            pltpu.VMEM((rows, w_out.shape[1]), BF16),
            pltpu.SemaphoreType.DMA((STORES,)),
        ],
        out_specs=[HBM],
        limit=20,
    )(send_order, returned, w_out)
    return out


def solution(mesh):
    return jax.shard_map(
        per_device,
        mesh=mesh,
        in_specs=(
            P(AXES, None),
            P(),
            P(),
            P(),
            P(),
            P(None, AXES),
            P(None, AXES),
        ),
        out_specs=P(AXES, None),
        check_vma=False,
    )
```
